256 devices in a mesh: section: 8 (over x, z_hi), dp: 4 (over y), expert: 8 (over z_lo, core).
Axes of the slice: x: 4, y: 4, z: 8 (z_hi: 2, z_lo: 4; z = z_hi * 4 + z_lo), core: 2. Of those that a mesh axis runs over, the one named last changes fastest.
Arguments:
- tokens: bfloat16 [8, 4096, 2560], P('section', ('dp', 'expert')), may hold values from -6 to 6
- cotangent: bfloat16 [8, 4096, 2560], P('section', ('dp', 'expert')), may hold values from -3 to 3
- routes: int32 [8, 4096, 6], P('section', ('dp', 'expert')), may hold values from 0 to 159, as said below
- gates: float32 [8, 4096, 6], P('section', ('dp', 'expert')), may hold values from 0.2 to 1
- gate_up: bfloat16 [8, 8, 2, 1024, 2560], P('section', 'expert', None, 'dp'), may hold values from -0.125 to 0.125
- down: bfloat16 [8, 8, 1024, 2560], P('section', 'expert', 'dp'), may hold values from -0.1875 to 0.1875
Outputs:
- handed_on: bfloat16 [8, 4096, 2560], P('section', ('dp', 'expert'))
- handed_back: bfloat16 [8, 4096, 2560], P('section', ('dp', 'expert'))
- grad_gate_up: bfloat16 [8, 8, 2, 1024, 2560], P('section', 'expert', None, 'dp')
- grad_down: bfloat16 [8, 8, 1024, 2560], P('section', 'expert', 'dp')
The draws below stay inside these ranges and needn't reach their ends.
Inputs may be any that keep to these rules, and one draw needn't show every extreme that they name: `routes`: A token's 6 ids are distinct and at most one of them is below 8. In each device's block of 128 tokens no id below 8 is named by more than 16 tokens.
All inputs are finite; a program needn't handle non-finite values.
Results may differ from the reference program's by a relative error of at most 0.0065.
Values may be sent and summed in bfloat16 or wider, within the bound.
A program may use at most 64 MiB of HBM per device.

```python
import jax
import jax.numpy as jnp
from jax import lax

D = 2560
H = 1024
EXPERTS_ALL = 160
TOP = 6
TOK_DEV = 128
SECTIONS = 8
WIN = 8
CAP = 16
ROWS = 4096
N_DP = 4
N_EXPERT = 8


def draw_routes(key, part):
    keys = jax.random.split(key, 5)
    labels = jnp.arange(WIN, dtype=jnp.int32)
    favoured = jax.random.randint(keys[0], (SECTIONS, N_DP, 1, 1), 0, WIN)
    counts = jax.random.randint(keys[1], (SECTIONS, N_DP, N_EXPERT, WIN), 0, CAP + 1)
    counts = jnp.where(labels == favoured, CAP, counts)
    starts = jnp.cumsum(counts, -1) - counts
    places = jnp.arange(TOK_DEV, dtype=jnp.int32)[:, None]
    inside = (places >= starts[..., None, :]) & (places < (starts + counts)[..., None, :])
    covered = jnp.any(inside, -1)
    owner = jnp.sum(jnp.where(inside, labels, 0), -1)
    scores = jax.random.randint(keys[2], (SECTIONS, N_DP, N_EXPERT, TOK_DEV), 0, 1 << 20) * TOK_DEV
    scores = scores + jnp.arange(TOK_DEV, dtype=jnp.int32)
    ordering = jnp.argsort(scores, -1)
    position = jnp.argsort(ordering, -1)
    row_owner = jnp.take_along_axis(owner, position, -1)
    row_covered = jnp.take_along_axis(covered, position, -1)
    outside = EXPERTS_ALL - WIN
    fills = jax.random.randint(keys[3], (SECTIONS, N_DP, N_EXPERT, TOK_DEV, outside), 0, 1 << 20) * 256
    fills = fills + jnp.arange(outside, dtype=jnp.int32)
    unused, picks = lax.top_k(fills, TOP)
    picks = picks.astype(jnp.int32) + WIN
    leading = jnp.where(row_covered, row_owner, picks[..., 0])
    chosen = jnp.concatenate([leading[..., None], picks[..., 1:]], -1)
    mixing = jax.random.randint(keys[4], (SECTIONS, N_DP, N_EXPERT, TOK_DEV, TOP), 0, 1 << 20) * 8
    mixing = mixing + jnp.arange(TOP, dtype=jnp.int32)
    shuffle = jnp.argsort(mixing, -1)
    routes = jnp.take_along_axis(chosen, shuffle, -1)
    return routes.reshape(SECTIONS, N_DP * N_EXPERT * TOK_DEV, TOP).astype(jnp.int32)


def level_of(stream_key, dims, cuts, least, top_value):
    gain, own = 1.0, jax.random.fold_in(stream_key, 6)
    for axis_at, shards_of in cuts:
        draws = jnp.exp(jax.random.uniform(jax.random.fold_in(own, axis_at), (shards_of,), jnp.float32, least / len(cuts), top_value / len(cuts)))
        gain = gain * jnp.repeat(draws, dims[axis_at] // shards_of).reshape([-1 if axis == axis_at else 1 for axis in range(len(dims))])
    return gain


def normal_values(rng, extent, width, limit, cuts=(), held_as=jnp.bfloat16):
    entries = width * jax.random.normal(rng, extent, jnp.float32)
    if cuts:
        entries = entries * level_of(rng, extent, cuts, -0.22, 0.18)
    return jnp.clip(entries, -limit, limit).astype(held_as)


def setup_inputs(seed: int = 0) -> dict:
    arg_keys = jax.random.split(jax.random.key(seed), 7)
    return {
        "tokens": normal_values(arg_keys[0], (SECTIONS, ROWS, D), 1.0, 6.0, ((0, 8), (1, 32))),
        "cotangent": normal_values(arg_keys[1], (SECTIONS, ROWS, D), 0.5, 3.0, ((0, 8), (1, 32))),
        "routes": draw_routes(jax.random.fold_in(arg_keys[6], 71), 0),
        "gates": jnp.clip(0.2 + 0.8 * jax.random.uniform(arg_keys[3], (SECTIONS, ROWS, TOP), jnp.float32) ** level_of(arg_keys[3], (SECTIONS, ROWS, TOP), ((0, 8), (1, 32)), -0.2, 0.2), 0.2, 1.0),
        "gate_up": normal_values(arg_keys[4], (SECTIONS, WIN, 2, H, D), D ** -0.5, 0.125, ((0, 8), (1, 8), (3, 4))),
        "down": normal_values(arg_keys[5], (SECTIONS, WIN, H, D), H ** -0.5, 0.1875, ((0, 8), (1, 8), (2, 4))),
    }


def expert_pass(operands):
    slot_rows, slot_grads, gate_up, down = operands
    quarter = H // N_DP
    row_count = slot_rows.shape[0]
    pre_gate = jnp.dot(slot_rows, gate_up[0].T, preferred_element_type=jnp.float32)
    pre_up = jnp.dot(slot_rows, gate_up[1].T, preferred_element_type=jnp.float32)
    sigmoid_gate = jax.nn.sigmoid(pre_gate)
    activated = pre_gate * sigmoid_gate
    hidden = (activated * pre_up).astype(jnp.bfloat16)
    hidden_split = hidden.astype(jnp.float32).reshape(row_count, N_DP, quarter)
    down_split = down.astype(jnp.float32).reshape(N_DP, quarter, D)
    parts = jnp.einsum("rqh,qhd->qrd", hidden_split, down_split)
    parts = lax.optimization_barrier(parts.astype(jnp.bfloat16))
    expert_out = jnp.sum(parts.astype(jnp.float32), 0).astype(jnp.bfloat16)
    hidden_grad = jnp.dot(slot_grads, down.T, preferred_element_type=jnp.float32)
    grad_down = jnp.dot(hidden.T, slot_grads, preferred_element_type=jnp.float32).astype(jnp.bfloat16)
    gate_slope = sigmoid_gate * (1.0 + pre_gate * (1.0 - sigmoid_gate))
    gate_grad = (hidden_grad * pre_up * gate_slope).astype(jnp.bfloat16)
    up_grad = (hidden_grad * activated).astype(jnp.bfloat16)
    grad_gate = jnp.dot(gate_grad.T, slot_rows, preferred_element_type=jnp.float32).astype(jnp.bfloat16)
    grad_up = jnp.dot(up_grad.T, slot_rows, preferred_element_type=jnp.float32).astype(jnp.bfloat16)
    weights_split = gate_up.astype(jnp.float32).reshape(2, N_DP, quarter, D)
    gate_split = gate_grad.astype(jnp.float32).reshape(row_count, N_DP, quarter)
    up_split = up_grad.astype(jnp.float32).reshape(row_count, N_DP, quarter)
    input_parts = jnp.einsum("rqh,qhd->qrd", gate_split, weights_split[0])
    input_parts = input_parts + jnp.einsum("rqh,qhd->qrd", up_split, weights_split[1])
    input_parts = lax.optimization_barrier(input_parts.astype(jnp.bfloat16))
    slot_input = jnp.sum(input_parts.astype(jnp.float32), 0).astype(jnp.bfloat16)
    return expert_out, slot_input, jnp.stack([grad_gate, grad_up]), grad_down


def section_pass(operands):
    tokens, cotangent, routes, gates, gate_up, down = operands
    blocks = N_DP * N_EXPERT
    capacity = TOK_DEV // N_EXPERT
    section_rows = tokens.shape[0]
    block_routes = routes.reshape(blocks, TOK_DEV, TOP)
    block_gates = gates.reshape(blocks, TOK_DEV, TOP)
    in_window = block_routes < N_EXPERT
    expert_of = jnp.sum(jnp.where(in_window, block_routes, 0), -1)
    present = jnp.any(in_window, -1)
    weight = jnp.sum(jnp.where(in_window, block_gates, 0.0), -1)
    member = ((expert_of[..., None] == jnp.arange(N_EXPERT)) & present[..., None]).astype(jnp.float32)
    before = jnp.cumsum(member, 1) - member
    slot_index = jnp.sum(before * member, -1)
    slot_values = jnp.arange(capacity).astype(jnp.float32)
    select = jnp.swapaxes(member, 1, 2)[:, :, None, :] * (slot_index[:, None, None, :] == slot_values[None, None, :, None])
    block_rows = tokens.astype(jnp.float32).reshape(blocks, TOK_DEV, D)
    slot_rows = jnp.einsum("bect,btd->ebcd", select, block_rows).astype(jnp.bfloat16)
    slot_rows = slot_rows.reshape(N_EXPERT, blocks * capacity, D)
    scaled = (cotangent.astype(jnp.float32).reshape(blocks, TOK_DEV, D) * weight[..., None]).astype(jnp.bfloat16)
    slot_grads = jnp.einsum("bect,btd->ebcd", select, scaled.astype(jnp.float32)).astype(jnp.bfloat16)
    slot_grads = slot_grads.reshape(N_EXPERT, blocks * capacity, D)
    expert_out, slot_input, grad_gate_up, grad_down = lax.map(expert_pass, (slot_rows, slot_grads, gate_up, down))
    expert_out = expert_out.astype(jnp.float32).reshape(N_EXPERT, blocks, capacity, D)
    mixture = jnp.einsum("bect,ebcd->btd", select, expert_out) * weight[..., None]
    slot_input = slot_input.astype(jnp.float32).reshape(N_EXPERT, blocks, capacity, D)
    input_grad = jnp.einsum("bect,ebcd->btd", select, slot_input).astype(jnp.bfloat16)
    mixture = mixture.astype(jnp.bfloat16).reshape(section_rows, D)
    return mixture, input_grad.reshape(section_rows, D), grad_gate_up, grad_down


def reference(tokens, cotangent, routes, gates, gate_up, down):
    mixture, input_grad, grad_gate_up, grad_down = lax.map(section_pass, (tokens, cotangent, routes, gates, gate_up, down))
    handed_on = jnp.concatenate([jnp.zeros_like(mixture[:1]), mixture[:-1]], 0)
    handed_back = jnp.concatenate([input_grad[1:], jnp.zeros_like(input_grad[:1])], 0)
    return handed_on, handed_back, grad_gate_up, grad_down
```

```python
import functools

import jax
import jax.numpy as jnp
from jax import lax
from jax.experimental import pallas as pl
from jax.experimental.pallas import tpu as pltpu
from jax.sharding import PartitionSpec as P

MESH = pl.DeviceIdType.MESH
F32 = jnp.float32
BF16 = jnp.bfloat16
NT = (((1,), (1,)), ((), ()))
COLS = 512
COPIES = 80


def flipped(index, bits):
    out = index
    for b in range(3):
        if bits >> b & 1:
            out = out + (1 << b) * (1 - 2 * ((index // (1 << b)) % 2))
    return out


def kernel(
    tok_hbm, cot_hbm, routes_ref, gates_ref, gu_hbm, dn_hbm,
    on_hbm, back_hbm, ggu_hbm, gdn_hbm,
    tok, cot, wgu, wdn, pk, xs, part, rdiag, rown, fin, rsec, metas, metar,
    act, bsl, hid_t, gr_t, ggu, gdn, outs, lsem, osem, ssem, rsem,
):
    s = lax.axis_index("section")
    q = lax.axis_index("dp")
    e = lax.axis_index("expert")
    nxt, prv = (s + 1) % 8, (s + 7) % 8
    up, dwn = (q + 1) % 4, (q + 3) % 4
    rows, width = tok.shape
    n_tiles = width // COLS

    barrier = pltpu.get_barrier_semaphore()
    peers = [(s, q, flipped(e, k)) for k in range(1, 8)]
    peers += [(s, up, e), (s, dwn, e)]
    peers += [(t, q, flipped(e, k)) for t in (nxt, prv) for k in range(8)]
    for peer in peers:
        pl.semaphore_signal(barrier, inc=1, device_id=peer, device_id_type=MESH)

    loads = [
        pltpu.make_async_copy(src, dst, lsem.at[i])
        for i, (src, dst) in enumerate(
            ((tok_hbm, tok), (cot_hbm, cot), (gu_hbm, wgu), (dn_hbm, wdn))
        )
    ]
    for load in loads:
        load.start()

    used = []

    def copy(src, dst, peer):
        i = len(used)
        c = pltpu.make_async_remote_copy(
            src_ref=src, dst_ref=dst, send_sem=ssem.at[i], recv_sem=rsem.at[i],
            device_id=peer, device_id_type=MESH,
        )
        used.append(c)
        return c

    def tiles(body):
        @pl.loop(0, n_tiles)
        def _(j):
            body(pl.ds(pl.multiple_of(j * COLS, COLS), COLS))

    def chunk(ref, t, r, c):
        return ref.at[t, pl.ds(r * rows + c * 32, 32)]

    sides = ((up, 3), (dwn, 1))
    zc = [
        [None] + [
            copy(pk.at[t, pl.ds(k * 16, 16)], xs.at[t, pl.ds(k * 16, 16)], (s, q, flipped(e, k)))
            for k in range(1, 8)
        ]
        for t in range(2)
    ]
    own = [
        [[copy(chunk(xs, t, 0, c), chunk(xs, t, r, c), (s, y, e)) for y, r in sides] for c in range(4)]
        for t in range(2)
    ]
    onward = [
        [
            copy(chunk(xs, t, 3, c), chunk(xs, t, 2, c), (s, up, e)) if c < 2
            else copy(chunk(xs, t, 1, c), chunk(xs, t, 2, c), (s, dwn, e))
            for c in range(4)
        ]
        for t in range(2)
    ]
    far = [
        [
            copy(chunk(part, t, 2, c), rdiag.at[t, pl.ds(c * 32, 32)], (s, (up, dwn)[c // 2], e))
            for c in range(4)
        ]
        for t in range(2)
    ]
    near = [
        [
            [
                copy(chunk(part, t, r, c), rown.at[t, side, pl.ds(c * 32, 32)], (s, y, e))
                for side, (y, r) in enumerate(((up, 1), (dwn, 3)))
            ]
            for c in range(4)
        ]
        for t in range(2)
    ]
    final = [
        [
            copy(fin.at[t, pl.ds(k * 16, 16)], rsec.at[t, pl.ds(k * 16, 16)], ((nxt, prv)[t], q, flipped(e, k)))
            for k in range(8)
        ]
        for t in range(2)
    ]
    meta = [copy(metas, metar.at[t], ((nxt, prv)[t], q, e)) for t in range(2)]
    assert len(used) == COPIES

    in_window = routes_ref[...] < 8
    expert_of = jnp.sum(jnp.where(in_window, routes_ref[...].astype(F32), 0.0), 1, keepdims=True)
    present = jnp.sum(jnp.where(in_window, 1.0, 0.0), 1, keepdims=True) > 0.5
    weight = jnp.sum(jnp.where(in_window, gates_ref[...], 0.0), 1, keepdims=True)
    lane = lax.broadcasted_iota(jnp.int32, (rows, rows), 1)
    sub = lax.broadcasted_iota(jnp.int32, (rows, rows), 0)
    member = jnp.where((expert_of == lane.astype(F32)) & present, 1.0, 0.0)
    earlier = jnp.where(lane < sub, 1.0, 0.0).astype(BF16)
    before = jnp.dot(earlier, member.astype(BF16), preferred_element_type=F32)
    slot = jnp.sum(before * member, 1, keepdims=True)
    column = expert_of.astype(jnp.int32) ^ e
    place = jnp.where(present, column.astype(F32) * 16.0 + slot, -1.0)
    place_t = jnp.broadcast_to(place, (rows, rows)).T
    metas[0:8, :] = place_t[0:8, :]
    metas[8:16, :] = jnp.broadcast_to(weight, (rows, rows)).T[0:8, :]
    select = jnp.where(place_t == sub.astype(F32), 1.0, 0.0).astype(BF16)

    loads[0].wait()

    @tiles
    def _(cols):
        packed = jnp.dot(select, tok[:, cols], preferred_element_type=F32).astype(BF16)
        pk[0, :, cols] = packed
        xs[0, 0:16, cols] = packed[0:16, :]

    pl.semaphore_wait(barrier, len(peers))
    for k in (2, 3, 4, 5, 6, 7, 1):
        zc[0][k].start()

    loads[1].wait()

    @tiles
    def _(cols):
        scaled = (cot[:, cols].astype(F32) * weight).astype(BF16)
        packed = jnp.dot(select, scaled, preferred_element_type=F32).astype(BF16)
        pk[1, :, cols] = packed
        xs[1, 0:16, cols] = packed[0:16, :]

    def own_chunk(t, c):
        for k in (2 * c, 2 * c + 1):
            if k:
                zc[t][k].wait_recv()
        for y in own[t][c]:
            y.start()

    def pass_on(t, c):
        own[t][c][0 if c < 2 else 1].wait_recv()
        onward[t][c].start()

    def forward(r):
        span = pl.ds(r * rows, rows)
        pre = lax.dot_general(xs[0, span, :], wgu[...], NT, preferred_element_type=F32)
        half = pre.shape[1] // 2
        gate, upper = pre[:, :half], pre[:, half:]
        sig = jax.nn.sigmoid(gate)
        activated = gate * sig
        act[span, :] = activated
        bsl[span, :] = upper * (sig * (1.0 + gate * (1.0 - sig)))
        hid = activated * upper
        hid_t[:, span] = hid.T.astype(BF16)
        hidden = hid.astype(BF16)

        @tiles
        def _(cols):
            part[0, span, cols] = jnp.dot(hidden, wdn[:, cols], preferred_element_type=F32).astype(BF16)

    def backward(r):
        span = pl.ds(r * rows, rows)
        hg = lax.dot_general(xs[1, span, :], wdn[...], NT, preferred_element_type=F32)
        gg, ug = hg * bsl[span, :], hg * act[span, :]
        half = hg.shape[1]
        gr_t[:half, span] = gg.T.astype(BF16)
        gr_t[half:, span] = ug.T.astype(BF16)
        gg, ug = gg.astype(BF16), ug.astype(BF16)

        @tiles
        def _(cols):
            both = jnp.dot(gg, wgu[:half, cols], preferred_element_type=F32)
            both += jnp.dot(ug, wgu[half:, cols], preferred_element_type=F32)
            part[1, span, cols] = both.astype(BF16)

    def send_sums(t):
        for c in (0, 2, 1, 3):
            far[t][c].start()
        for c in range(2):
            near[t][2 + c][0].start()
            near[t][c][1].start()

    def merge(t):
        for c in (0, 2, 1, 3):
            far[t][c].wait_recv()
            r = 1 if c < 2 else 3
            mine, theirs = pl.ds(r * rows + c * 32, 32), pl.ds(c * 32, 32)

            @tiles
            def _(cols):
                total = part[t, mine, cols].astype(F32) + rdiag[t, theirs, cols].astype(F32)
                part[t, mine, cols] = total.astype(BF16)

            near[t][c][0 if c < 2 else 1].start()

    def finish(t, c):
        for y in near[t][c]:
            y.wait_recv()
        span = pl.ds(c * 32, 32)

        @tiles
        def _(cols):
            total = part[t, span, cols].astype(F32) + rown[t, 0, span, cols].astype(F32)
            fin[t, span, cols] = (total + rown[t, 1, span, cols].astype(F32)).astype(BF16)

        for k in (2 * c, 2 * c + 1):
            final[t][k].start()

    own_chunk(0, 0)
    own_chunk(0, 1)
    pass_on(0, 0)
    own_chunk(0, 2)
    pass_on(0, 1)
    own_chunk(0, 3)
    for k in (2, 3, 4, 5, 6, 7, 1):
        zc[1][k].start()
    for m in meta:
        m.start()
    pass_on(0, 2)
    pass_on(0, 3)
    own_chunk(1, 0)
    loads[2].wait()
    loads[3].wait()
    forward(0)
    own_chunk(1, 1)
    own[0][0][1].wait_recv()
    own[0][1][1].wait_recv()
    own[0][2][0].wait_recv()
    own[0][3][0].wait_recv()
    forward(1)
    own_chunk(1, 2)
    pass_on(1, 0)
    forward(3)
    own_chunk(1, 3)
    pass_on(1, 1)
    for c in range(4):
        onward[0][c].wait_recv()
    forward(2)
    send_sums(0)
    pass_on(1, 2)
    pass_on(1, 3)
    backward(0)
    own[1][0][1].wait_recv()
    own[1][1][1].wait_recv()
    own[1][2][0].wait_recv()
    own[1][3][0].wait_recv()
    backward(1)
    merge(0)
    backward(3)
    for c in range(4):
        onward[1][c].wait_recv()
    backward(2)
    send_sums(1)
    for c in range(4):
        finish(0, c)
    merge(1)

    @pl.loop(0, n_tiles)
    def _(j):
        cols = pl.ds(pl.multiple_of(j * COLS, COLS), COLS)
        gdn[:, cols] = jnp.dot(hid_t[...], xs[1, :, cols], preferred_element_type=F32).astype(BF16)

    stores = [
        pltpu.make_async_copy(src, dst, osem.at[i])
        for i, (src, dst) in enumerate(
            ((gdn, gdn_hbm), (ggu, ggu_hbm), (outs.at[0], on_hbm), (outs.at[1], back_hbm))
        )
    ]
    stores[0].start()
    for c in range(4):
        finish(1, c)

    @pl.loop(0, n_tiles)
    def _(j):
        cols = pl.ds(pl.multiple_of(j * COLS, COLS), COLS)
        half = ggu.shape[0] // 2
        for top in (0, half):
            span = pl.ds(top, half)
            ggu[span, cols] = jnp.dot(gr_t[span, :], xs[0, :, cols], preferred_element_type=F32).astype(BF16)

    stores[1].start()

    for t in range(2):
        meta[t].wait_recv()
        there = jnp.broadcast_to(metar[t, 0:1, :], (rows, rows)).T
        pick = jnp.where(there == lane.astype(F32), 1.0, 0.0).astype(BF16)
        scale = jnp.broadcast_to(metar[t, 8:9, :], (rows, rows)).T[:, 0:1]
        edge = s == (0, 7)[t]
        for k in range(8):
            final[t][k].wait_recv()

        @tiles
        def _(cols):
            mixed = jnp.dot(pick, rsec[t, :, cols], preferred_element_type=F32)
            if t == 0:
                mixed = mixed * scale
            outs[t, :, cols] = jnp.where(edge, 0.0, mixed).astype(BF16)

        stores[2 + t].start()

    for c in used:
        c.wait_send()
    for store in stores:
        store.wait()


def shards(tokens, cotangent, routes, gates, gate_up, down):
    rows, width = tokens.shape[1:]
    quarter = down.shape[2]
    both = 2 * quarter
    hbm = pl.BlockSpec(memory_space=pl.ANY)
    vmem = pl.BlockSpec(memory_space=pltpu.VMEM)
    shape = lambda *dims: jax.ShapeDtypeStruct(dims, BF16)
    flops = 2 * 9 * 4 * rows * quarter * width
    on, back, ggu, gdn = pl.pallas_call(
        kernel,
        out_shape=(shape(rows, width), shape(rows, width), shape(both, width), shape(quarter, width)),
        in_specs=[hbm, hbm, vmem, vmem, hbm, hbm],
        out_specs=[hbm] * 4,
        scratch_shapes=[
            pltpu.VMEM((rows, width), BF16),
            pltpu.VMEM((rows, width), BF16),
            pltpu.VMEM((both, width), BF16),
            pltpu.VMEM((quarter, width), BF16),
            pltpu.VMEM((2, rows, width), BF16),
            pltpu.VMEM((2, 4 * rows, width), BF16),
            pltpu.VMEM((2, 4 * rows, width), BF16),
            pltpu.VMEM((2, rows, width), BF16),
            pltpu.VMEM((2, 2, rows, width), BF16),
            pltpu.VMEM((2, rows, width), BF16),
            pltpu.VMEM((2, rows, width), BF16),
            pltpu.VMEM((16, rows), F32),
            pltpu.VMEM((2, 16, rows), F32),
            pltpu.VMEM((4 * rows, quarter), F32),
            pltpu.VMEM((4 * rows, quarter), F32),
            pltpu.VMEM((quarter, 4 * rows), BF16),
            pltpu.VMEM((both, 4 * rows), BF16),
            pltpu.VMEM((both, width), BF16),
            pltpu.VMEM((quarter, width), BF16),
            pltpu.VMEM((2, rows, width), BF16),
            pltpu.SemaphoreType.DMA((4,)),
            pltpu.SemaphoreType.DMA((4,)),
            pltpu.SemaphoreType.DMA((COPIES,)),
            pltpu.SemaphoreType.DMA((COPIES,)),
        ],
        compiler_params=pltpu.CompilerParams(
            collective_id=0, has_side_effects=True, vmem_limit_bytes=56 * 2**20
        ),
        cost_estimate=pl.CostEstimate(flops=flops, bytes_accessed=12 * 2**20, transcendentals=0),
    )(
        tokens[0], cotangent[0], routes[0], gates[0],
        gate_up.reshape(both, width), down.reshape(quarter, width),
    )
    return (
        on[None],
        back[None],
        ggu.reshape(gate_up.shape),
        gdn.reshape(down.shape),
    )


def solution(mesh):
    in_specs = (
        P("section", ("dp", "expert"), None),
        P("section", ("dp", "expert"), None),
        P("section", ("dp", "expert"), None),
        P("section", ("dp", "expert"), None),
        P("section", "expert", None, "dp", None),
        P("section", "expert", "dp", None),
    )
    out_specs = (
        P("section", ("dp", "expert"), None),
        P("section", ("dp", "expert"), None),
        P("section", "expert", None, "dp", None),
        P("section", "expert", "dp", None),
    )
    return jax.shard_map(shards, mesh=mesh, in_specs=in_specs, out_specs=out_specs, check_vma=False)
```

```python
import functools

import jax
import jax.numpy as jnp
from jax import lax
from jax.experimental import pallas as pl
from jax.experimental.pallas import tpu as pltpu
from jax.sharding import PartitionSpec as P

MESH = pl.DeviceIdType.MESH
F32 = jnp.float32
BF16 = jnp.bfloat16
NT = (((1,), (1,)), ((), ()))
COLS = 512
WIDE = 640
PIECES = ((0,), (1,), (2,), (3,), (4,), (5,), (6,), (7,))
COPIES = 7 + 10 * len(PIECES) + 16 + 2
ORDER = (
    "Z1", "Z2", "Z3", "Z4", "Z5", "Z6", "Z7", "A0", "A1", "B0", "P0", "A2",
    "B1", "C0", "R0", "A3", "M0", "B2", "C1", "R1", "F0", "A4", "M1", "B3",
    "C2", "R2", "F1", "A5", "M2", "B4", "C3", "R3", "F2", "A6", "M3", "B5",
    "C4", "R4", "F3", "A7", "M4", "B6", "C5", "R5", "F4", "M5", "B7", "C6",
    "R6", "F5", "M6", "C7", "R7", "F6", "D0", "M7", "F7", "G0",
)


def flipped(index, bits):
    out = index
    for b in range(3):
        if bits >> b & 1:
            out = out + (1 << b) * (1 - 2 * ((index // (1 << b)) % 2))
    return out


def kernel(
    tok_hbm, cot_hbm, routes_hbm, gates_hbm, gu_hbm, dn_hbm,
    rsec, metar, ggu, gdn,
    tok, cot, wgu, wdn, routes_ref, gates_ref, pk, xs, part, rdiag, rown, fin, metas,
    hid, gr, lsem, ssem, rsem,
):
    s = lax.axis_index("section")
    q = lax.axis_index("dp")
    e = lax.axis_index("expert")
    nxt, prv = (s + 1) % 8, (s + 7) % 8
    up, dwn = (q + 1) % 4, (q + 3) % 4
    rows, width = tok.shape
    quarter = wdn.shape[0]
    left, right = pl.ds(0, width // 2), pl.ds(width // 2, width // 2)

    barrier = pltpu.get_barrier_semaphore()
    peers = [(s, q, flipped(e, k)) for k in range(1, 8)]
    peers += [(s, up, e), (s, dwn, e)]
    peers += [(t, q, flipped(e, k)) for t in (nxt, prv) for k in range(8)]
    for peer in peers:
        pl.semaphore_signal(barrier, inc=1, device_id=peer, device_id_type=MESH)

    loads = [
        pltpu.make_async_copy(src, dst, lsem.at[i])
        for i, (src, dst) in enumerate(
            (
                (tok_hbm, tok), (cot_hbm, cot), (gu_hbm, wgu), (dn_hbm, wdn),
                (routes_hbm, routes_ref), (gates_hbm, gates_ref),
            )
        )
    ]
    for i in (4, 5, 0, 1, 2, 3):
        loads[i].start()
    used = []

    def copy(src, dst, peer):
        i = len(used)
        c = pltpu.make_async_remote_copy(
            src_ref=src, dst_ref=dst, send_sem=ssem.at[i], recv_sem=rsem.at[i],
            device_id=peer, device_id_type=MESH,
        )
        used.append(c)
        return c

    def tiles(body, first=0, last=width, step=COLS):
        @pl.loop(first // step, last // step)
        def _(j):
            body(pl.ds(pl.multiple_of(j * step, step), step))

    start = [64 * sum(len(p) for p in PIECES[:c]) for c in range(len(PIECES))]
    size = [16 * len(p) for p in PIECES]

    def block(r, c):
        return pl.ds(start[c] + r * size[c], size[c])

    def slots(c):
        return pl.ds(16 * PIECES[c][0], size[c])

    both = pl.ds(0, 2)
    zc = {}
    own, onward, far, near, merged, final = [], [], [], [], [], {}
    for c, piece in enumerate(PIECES):
        for i, k in enumerate(piece):
            at = pl.ds(start[c] + 16 * i, 16)
            if k:
                zc[k] = copy(pk.at[both, pl.ds(k * 16, 16)], xs.at[both, at], (s, q, flipped(e, k)))
    for c in range(len(PIECES)):
        own.append([copy(xs.at[both, block(0, c)], xs.at[both, block(r, c)], (s, y, e)) for y, r in ((up, 3), (dwn, 1))])
        onward.append([
            copy(xs.at[both, block(r, c), h], xs.at[both, block(2, c), h], (s, y, e))
            for y, r, h in ((up, 3, left), (dwn, 1, right))
        ])
        far.append([
            copy(part.at[both, block(2, c), h], rdiag.at[both, slots(c), h], (s, y, e))
            for y, h in ((up, left), (dwn, right))
        ])
        near.append([
            copy(part.at[both, block(r, c), h], rown.at[i, both, slots(c), h], (s, y, e))
            for i, (y, r, h) in enumerate(((up, 1, right), (dwn, 3, left)))
        ])
        merged.append([
            copy(part.at[both, block(r, c), h], rown.at[i, both, slots(c), h], (s, y, e))
            for i, (y, r, h) in enumerate(((up, 1, left), (dwn, 3, right)))
        ])
    for t in range(2):
        for k in range(8):
            at = pl.ds(k * 16, 16)
            final[t, k] = copy(fin.at[t, at], rsec.at[t, at], ((nxt, prv)[t], q, flipped(e, k)))
    meta = [copy(metas, metar.at[t], ((nxt, prv)[t], q, e)) for t in range(2)]
    assert len(used) == COPIES

    loads[4].wait()
    loads[5].wait()
    in_window = routes_ref[...] < 8
    expert_of = jnp.sum(jnp.where(in_window, routes_ref[...], 0), 0)
    present = jnp.sum(jnp.where(in_window, 1, 0), 0) > 0
    weight = jnp.sum(jnp.where(in_window, gates_ref[...], 0.0), 0)
    lane = lax.broadcasted_iota(jnp.int32, (rows, rows), 1)
    sub = lax.broadcasted_iota(jnp.int32, (rows, rows), 0)
    member = jnp.where((expert_of == sub[0:16]) & present, 1.0, 0.0)
    earlier = jnp.where(sub < lane, 1.0, 0.0).astype(BF16)
    before = jnp.dot(member.astype(BF16), earlier, preferred_element_type=F32)
    slot = jnp.sum(before * member, 0, keepdims=True)
    column = expert_of ^ e
    place = jnp.where(present, column.astype(F32) * 16.0 + slot, -1.0)
    metas[0:8, :] = jnp.broadcast_to(place, (8, rows))
    metas[8:16, :] = jnp.broadcast_to(weight, (8, rows))
    select = jnp.where(place == sub.astype(F32), 1.0, 0.0).astype(BF16)
    scale_here = jnp.broadcast_to(weight, (rows, rows)).T[:, 0:1]

    for t in range(2):
        loads[t].wait()

        @tiles
        def _(cols):
            values = tok[:, cols] if t == 0 else (cot[:, cols].astype(F32) * scale_here).astype(BF16)
            packed = jnp.dot(select, values, preferred_element_type=F32).astype(BF16)
            pk[t, :, cols] = packed
            xs[t, 0:16, cols] = packed[0:16, :]

    pl.semaphore_wait(barrier, len(peers))

    def send_out(c):
        for k in PIECES[c]:
            if k:
                zc[k].start()

    def spread(c):
        for k in PIECES[c]:
            if k:
                zc[k].wait_recv()
        for y in own[c]:
            y.start()

    def pass_on(c):
        for i in range(2):
            own[c][i].wait_recv()
            onward[c][i].start()

    def compute(c):
        for y in onward[c]:
            y.wait_recv()
        span = pl.ds(start[c], 4 * size[c])
        pre = lax.dot_general(xs[0, span, :], wgu[...], NT, preferred_element_type=F32)
        gate, upper = pre[:, :quarter], pre[:, quarter:]
        sig = jax.nn.sigmoid(gate)
        activated = gate * sig
        hidden = activated * upper
        hid[span, :] = hidden
        hidden = hidden.astype(BF16)
        hg = lax.dot_general(xs[1, span, :], wdn[...], NT, preferred_element_type=F32)
        gg = hg * upper * (sig * (1.0 + gate * (1.0 - sig)))
        ug = hg * activated
        gr[span, :quarter] = gg
        gr[span, quarter:] = ug
        gg, ug = gg.astype(BF16), ug.astype(BF16)

        @tiles
        def _(cols):
            part[0, span, cols] = jnp.dot(hidden, wdn[:, cols], preferred_element_type=F32).astype(BF16)
            into = jnp.dot(gg, wgu[:quarter, cols], preferred_element_type=F32)
            into += jnp.dot(ug, wgu[quarter:, cols], preferred_element_type=F32)
            part[1, span, cols] = into.astype(BF16)

    def reduce(c):
        for y in (*far[c], *near[c]):
            y.start()

    def merge(c):
        for i, (r, first, last) in enumerate(((1, 0, width // 2), (3, width // 2, width))):
            far[c][i].wait_recv()
            mine, theirs = block(r, c), slots(c)

            @functools.partial(tiles, first=first, last=last, step=WIDE)
            def _(cols):
                for t in range(2):
                    total = part[t, mine, cols].astype(F32) + rdiag[t, theirs, cols].astype(F32)
                    part[t, mine, cols] = total.astype(BF16)

            merged[c][i].start()

    def finish(c):
        for y in (*near[c], *merged[c]):
            y.wait_recv()
        mine, span = block(0, c), slots(c)

        @functools.partial(tiles, step=WIDE)
        def _(cols):
            for t in range(2):
                total = part[t, mine, cols].astype(F32) + rown[0, t, span, cols].astype(F32)
                fin[t, span, cols] = (total + rown[1, t, span, cols].astype(F32)).astype(BF16)

        for k in PIECES[c]:
            for t in range(2):
                final[t, k].start()

    def grad_down(_):
        flat = hid[...].T.astype(BF16)

        @tiles
        def _(cols):
            gdn[:, cols] = jnp.dot(flat, xs[1, :, cols], preferred_element_type=F32).astype(BF16)


    def grad_gate_up(_):
        for top in (0, quarter):
            flat = gr[:, top : top + quarter].T.astype(BF16)

            @tiles
            def _(cols):
                ggu[top : top + quarter, cols] = jnp.dot(flat, xs[0, :, cols], preferred_element_type=F32).astype(BF16)


    def ready(_):
        for m in meta:
            m.start()
        for load in loads[2:4]:
            load.wait()

    steps = {
        "Z": send_out, "A": spread, "B": pass_on, "C": compute, "R": reduce, "M": merge, "F": finish,
        "D": grad_down, "G": grad_gate_up, "P": ready,
    }
    for step in ORDER:
        steps[step[0]](int(step[1:]))

    for c in (*meta, *final.values()):
        c.wait_recv()
    for c in used:
        c.wait_send()


def place_rows(slots, metar, ggu, gdn, on_hbm, back_hbm, ggu_hbm, gdn_hbm, outs, sems):
    s = lax.axis_index("section")
    rows, width = on_hbm.shape
    gives = [
        pltpu.make_async_copy(src, dst, sems.at[i])
        for i, (src, dst) in enumerate(
            ((outs.at[0], on_hbm), (outs.at[1], back_hbm), (ggu, ggu_hbm), (gdn, gdn_hbm))
        )
    ]
    for give in gives[2:]:
        give.start()
    lane = lax.broadcasted_iota(jnp.int32, (rows, rows), 1)
    for t in range(2):
        there = jnp.broadcast_to(metar[t, 0:1, :], (rows, rows)).T
        pick = jnp.where(there == lane.astype(F32), 1.0, 0.0).astype(BF16)
        scale = jnp.broadcast_to(metar[t, 8:9, :], (rows, rows)).T[:, 0:1]
        edge = s == (0, 7)[t]

        @pl.loop(0, width // COLS)
        def _(j):
            cols = pl.ds(pl.multiple_of(j * COLS, COLS), COLS)
            mixed = jnp.dot(pick, slots[t, :, cols], preferred_element_type=F32)
            if t == 0:
                mixed = mixed * scale
            outs[t, :, cols] = jnp.where(edge, 0.0, mixed).astype(BF16)

        gives[t].start()
    for give in gives:
        give.wait()


def shards(tokens, cotangent, routes, gates, gate_up, down):
    rows, width = tokens.shape[1:]
    quarter = down.shape[2]
    both = 2 * quarter
    hbm = pl.BlockSpec(memory_space=pl.ANY)
    in_hbm = lambda x: pltpu.with_memory_space_constraint(x, pltpu.HBM)
    vmem = pl.BlockSpec(memory_space=pltpu.VMEM)
    shape = lambda *dims: jax.ShapeDtypeStruct(dims, BF16)
    flops = 2 * 9 * 4 * rows * quarter * width
    handed, metar, ggu, gdn = pl.pallas_call(
        kernel,
        out_shape=(
            pltpu.VMEM((2, rows, width), BF16),
            pltpu.VMEM((2, 16, rows), F32),
            pltpu.VMEM((both, width), BF16),
            pltpu.VMEM((quarter, width), BF16),
        ),
        in_specs=[hbm] * 6,
        out_specs=[vmem] * 4,
        scratch_shapes=[
            pltpu.VMEM((rows, width), BF16),
            pltpu.VMEM((rows, width), BF16),
            pltpu.VMEM((both, width), BF16),
            pltpu.VMEM((quarter, width), BF16),
            pltpu.VMEM((6, 1, rows), jnp.int32),
            pltpu.VMEM((6, 1, rows), F32),
            pltpu.VMEM((2, rows, width), BF16),
            pltpu.VMEM((2, 4 * rows, width), BF16),
            pltpu.VMEM((2, 4 * rows, width), BF16),
            pltpu.VMEM((2, rows, width), BF16),
            pltpu.VMEM((2, 2, rows, width), BF16),
            pltpu.VMEM((2, rows, width), BF16),
            pltpu.VMEM((16, rows), F32),
            pltpu.VMEM((4 * rows, quarter), F32),
            pltpu.VMEM((4 * rows, both), F32),
            pltpu.SemaphoreType.DMA((6,)),
            pltpu.SemaphoreType.DMA((COPIES,)),
            pltpu.SemaphoreType.DMA((COPIES,)),
        ],
        compiler_params=pltpu.CompilerParams(
            collective_id=0, has_side_effects=True, vmem_limit_bytes=40 * 2**20
        ),
        cost_estimate=pl.CostEstimate(flops=flops, bytes_accessed=12 * 2**20, transcendentals=0),
    )(
        in_hbm(tokens[0]), in_hbm(cotangent[0]),
        in_hbm(routes.transpose(2, 0, 1)), in_hbm(gates.transpose(2, 0, 1)),
        in_hbm(gate_up.reshape(both, width)), in_hbm(down.reshape(quarter, width)),
    )
    on, back, ggu, gdn = pl.pallas_call(
        place_rows,
        out_shape=(shape(rows, width), shape(rows, width), shape(both, width), shape(quarter, width)),
        in_specs=[vmem] * 4,
        out_specs=[hbm] * 4,
        scratch_shapes=[pltpu.VMEM((2, rows, width), BF16), pltpu.SemaphoreType.DMA((4,))],
        compiler_params=pltpu.CompilerParams(vmem_limit_bytes=24 * 2**20),
        cost_estimate=pl.CostEstimate(flops=8 * 128 * rows * width, bytes_accessed=11 * 2**20, transcendentals=0),
    )(*(pltpu.with_memory_space_constraint(x, pltpu.VMEM) for x in (handed, metar, ggu, gdn)))
    return (
        on[None],
        back[None],
        ggu.reshape(gate_up.shape),
        gdn.reshape(down.shape),
    )


def solution(mesh):
    in_specs = (
        P("section", ("dp", "expert"), None),
        P("section", ("dp", "expert"), None),
        P("section", ("dp", "expert"), None),
        P("section", ("dp", "expert"), None),
        P("section", "expert", None, "dp", None),
        P("section", "expert", "dp", None),
    )
    out_specs = (
        P("section", ("dp", "expert"), None),
        P("section", ("dp", "expert"), None),
        P("section", "expert", None, "dp", None),
        P("section", "expert", "dp", None),
    )
    return jax.shard_map(shards, mesh=mesh, in_specs=in_specs, out_specs=out_specs, check_vma=False)
```

```python
import functools

import jax
import jax.numpy as jnp
from jax import lax
from jax.experimental import pallas as pl
from jax.experimental.pallas import tpu as pltpu
from jax.sharding import PartitionSpec as P

MESH = pl.DeviceIdType.MESH
F32 = jnp.float32
BF16 = jnp.bfloat16
NT = (((1,), (1,)), ((), ()))
COLS = 512
WIDE = 640
PIECES = ((0,), (1,), (2,), (3,), (4,), (5,), (6,), (7,))
COPIES = 7 + 10 * len(PIECES) + 16 + 2
ORDER = (
    "Z1", "Z2", "Z3", "Z4", "Z5", "Z6", "Z7", "A0", "A1", "B0", "P0", "A2",
    "B1", "C0", "R0", "M0", "A3", "B2", "C1", "R1", "F0", "M1", "A4", "B3",
    "C2", "R2", "F1", "M2", "A5", "B4", "C3", "R3", "F2", "M3", "A6", "B5",
    "C4", "R4", "F3", "M4", "A7", "B6", "C5", "R5", "F4", "M5", "B7", "C6",
    "R6", "F5", "M6", "C7", "R7", "F6", "D0", "M7", "F7", "G0",
)


def flipped(index, bits):
    out = index
    for b in range(3):
        if bits >> b & 1:
            out = out + (1 << b) * (1 - 2 * ((index // (1 << b)) % 2))
    return out


def kernel(
    tok_hbm, cot_hbm, routes_hbm, gates_hbm, gu_hbm, dn_hbm,
    rsec, metar, ggu, gdn,
    tok, cot, wgu, wdn, routes_ref, gates_ref, pk, xs, part, rdiag, rown, fin, metas,
    hid, gr, lsem, ssem, rsem,
):
    s = lax.axis_index("section")
    q = lax.axis_index("dp")
    e = lax.axis_index("expert")
    nxt, prv = (s + 1) % 8, (s + 7) % 8
    up, dwn = (q + 1) % 4, (q + 3) % 4
    rows, width = tok.shape
    quarter = wdn.shape[0]
    left, right = pl.ds(0, width // 2), pl.ds(width // 2, width // 2)

    barrier = pltpu.get_barrier_semaphore()
    peers = [(s, q, flipped(e, k)) for k in range(1, 8)]
    peers += [(s, up, e), (s, dwn, e)]
    peers += [(t, q, flipped(e, k)) for t in (nxt, prv) for k in range(8)]
    for peer in peers:
        pl.semaphore_signal(barrier, inc=1, device_id=peer, device_id_type=MESH)

    loads = [
        pltpu.make_async_copy(src, dst, lsem.at[i])
        for i, (src, dst) in enumerate(
            (
                (tok_hbm, tok), (cot_hbm, cot), (gu_hbm, wgu), (dn_hbm, wdn),
                (routes_hbm, routes_ref), (gates_hbm, gates_ref),
            )
        )
    ]
    for i in (4, 5, 0, 1, 2, 3):
        loads[i].start()
    used = []

    def copy(src, dst, peer):
        i = len(used)
        c = pltpu.make_async_remote_copy(
            src_ref=src, dst_ref=dst, send_sem=ssem.at[i], recv_sem=rsem.at[i],
            device_id=peer, device_id_type=MESH,
        )
        used.append(c)
        return c

    def tiles(body, first=0, last=width, step=COLS):
        @pl.loop(first // step, last // step)
        def _(j):
            body(pl.ds(pl.multiple_of(j * step, step), step))

    start = [64 * sum(len(p) for p in PIECES[:c]) for c in range(len(PIECES))]
    size = [16 * len(p) for p in PIECES]

    def block(r, c):
        return pl.ds(start[c] + r * size[c], size[c])

    def slots(c):
        return pl.ds(16 * PIECES[c][0], size[c])

    both = pl.ds(0, 2)
    zc = {}
    own, onward, far, near, merged, final = [], [], [], [], [], {}
    for c, piece in enumerate(PIECES):
        for i, k in enumerate(piece):
            at = pl.ds(start[c] + 16 * i, 16)
            if k:
                zc[k] = copy(pk.at[both, pl.ds(k * 16, 16)], xs.at[both, at], (s, q, flipped(e, k)))
    for c in range(len(PIECES)):
        own.append([copy(xs.at[both, block(0, c)], xs.at[both, block(r, c)], (s, y, e)) for y, r in ((up, 3), (dwn, 1))])
        onward.append([
            copy(xs.at[both, block(r, c), h], xs.at[both, block(2, c), h], (s, y, e))
            for y, r, h in ((up, 3, left), (dwn, 1, right))
        ])
        far.append([
            copy(part.at[both, block(2, c), h], rdiag.at[both, slots(c), h], (s, y, e))
            for y, h in ((up, left), (dwn, right))
        ])
        near.append([
            copy(part.at[both, block(r, c), h], rown.at[i, both, slots(c), h], (s, y, e))
            for i, (y, r, h) in enumerate(((up, 1, right), (dwn, 3, left)))
        ])
        merged.append([
            copy(part.at[both, block(r, c), h], rown.at[i, both, slots(c), h], (s, y, e))
            for i, (y, r, h) in enumerate(((up, 1, left), (dwn, 3, right)))
        ])
    for t in range(2):
        for k in range(8):
            at = pl.ds(k * 16, 16)
            final[t, k] = copy(fin.at[t, at], rsec.at[t, at], ((nxt, prv)[t], q, flipped(e, k)))
    meta = [copy(metas, metar.at[t], ((nxt, prv)[t], q, e)) for t in range(2)]
    assert len(used) == COPIES

    loads[4].wait()
    loads[5].wait()
    in_window = routes_ref[...] < 8
    expert_of = jnp.sum(jnp.where(in_window, routes_ref[...], 0), 0)
    present = jnp.sum(jnp.where(in_window, 1, 0), 0) > 0
    weight = jnp.sum(jnp.where(in_window, gates_ref[...], 0.0), 0)
    lane = lax.broadcasted_iota(jnp.int32, (rows, rows), 1)
    sub = lax.broadcasted_iota(jnp.int32, (rows, rows), 0)
    member = jnp.where((expert_of == sub[0:16]) & present, 1.0, 0.0)
    earlier = jnp.where(sub < lane, 1.0, 0.0).astype(BF16)
    before = jnp.dot(member.astype(BF16), earlier, preferred_element_type=F32)
    slot = jnp.sum(before * member, 0, keepdims=True)
    column = expert_of ^ e
    place = jnp.where(present, column.astype(F32) * 16.0 + slot, -1.0)
    metas[0:8, :] = jnp.broadcast_to(place, (8, rows))
    metas[8:16, :] = jnp.broadcast_to(weight, (8, rows))
    select = jnp.where(place == sub.astype(F32), 1.0, 0.0).astype(BF16)
    scale_here = jnp.broadcast_to(weight, (rows, rows)).T[:, 0:1]

    for t in range(2):
        loads[t].wait()

        @tiles
        def _(cols):
            values = tok[:, cols] if t == 0 else (cot[:, cols].astype(F32) * scale_here).astype(BF16)
            packed = jnp.dot(select, values, preferred_element_type=F32).astype(BF16)
            pk[t, :, cols] = packed
            xs[t, 0:16, cols] = packed[0:16, :]

    pl.semaphore_wait(barrier, len(peers))

    def send_out(c):
        for k in PIECES[c]:
            if k:
                zc[k].start()

    def spread(c):
        for k in PIECES[c]:
            if k:
                zc[k].wait_recv()
        for y in own[c]:
            y.start()

    def pass_on(c):
        for i in range(2):
            own[c][i].wait_recv()
            onward[c][i].start()

    def compute(c):
        for y in onward[c]:
            y.wait_recv()
        span = pl.ds(start[c], 4 * size[c])
        pre = lax.dot_general(xs[0, span, :], wgu[...], NT, preferred_element_type=F32)
        gate, upper = pre[:, :quarter], pre[:, quarter:]
        sig = jax.nn.sigmoid(gate)
        activated = gate * sig
        hidden = activated * upper
        hid[span, :] = hidden
        hidden = hidden.astype(BF16)
        hg = lax.dot_general(xs[1, span, :], wdn[...], NT, preferred_element_type=F32)
        gg = hg * upper * (sig * (1.0 + gate * (1.0 - sig)))
        ug = hg * activated
        gr[span, :quarter] = gg
        gr[span, quarter:] = ug
        gg, ug = gg.astype(BF16), ug.astype(BF16)

        @tiles
        def _(cols):
            part[0, span, cols] = jnp.dot(hidden, wdn[:, cols], preferred_element_type=F32).astype(BF16)
            into = jnp.dot(gg, wgu[:quarter, cols], preferred_element_type=F32)
            into += jnp.dot(ug, wgu[quarter:, cols], preferred_element_type=F32)
            part[1, span, cols] = into.astype(BF16)

    def reduce(c):
        for y in (*far[c], *near[c]):
            y.start()

    def merge(c):
        for i, (r, first, last) in enumerate(((1, 0, width // 2), (3, width // 2, width))):
            far[c][i].wait_recv()
            mine, theirs = block(r, c), slots(c)

            @functools.partial(tiles, first=first, last=last, step=WIDE)
            def _(cols):
                for t in range(2):
                    total = part[t, mine, cols].astype(F32) + rdiag[t, theirs, cols].astype(F32)
                    part[t, mine, cols] = total.astype(BF16)

            merged[c][i].start()

    def finish(c):
        for y in (*near[c], *merged[c]):
            y.wait_recv()
        mine, span = block(0, c), slots(c)

        @functools.partial(tiles, step=WIDE)
        def _(cols):
            for t in range(2):
                total = part[t, mine, cols].astype(F32) + rown[0, t, span, cols].astype(F32)
                fin[t, span, cols] = (total + rown[1, t, span, cols].astype(F32)).astype(BF16)

        for k in PIECES[c]:
            for t in range(2):
                final[t, k].start()

    def grad_down(_):
        flat = hid[...].T.astype(BF16)

        @tiles
        def _(cols):
            gdn[:, cols] = jnp.dot(flat, xs[1, :, cols], preferred_element_type=F32).astype(BF16)


    def grad_gate_up(_):
        for top in (0, quarter):
            flat = gr[:, top : top + quarter].T.astype(BF16)

            @tiles
            def _(cols):
                ggu[top : top + quarter, cols] = jnp.dot(flat, xs[0, :, cols], preferred_element_type=F32).astype(BF16)


    def ready(_):
        for m in meta:
            m.start()
        for load in loads[2:4]:
            load.wait()

    steps = {
        "Z": send_out, "A": spread, "B": pass_on, "C": compute, "R": reduce, "M": merge, "F": finish,
        "D": grad_down, "G": grad_gate_up, "P": ready,
    }
    for step in ORDER:
        steps[step[0]](int(step[1:]))

    for c in (*meta, *final.values()):
        c.wait_recv()
    for c in used:
        c.wait_send()


def place_rows(slots, metar, ggu, gdn, on_hbm, back_hbm, ggu_hbm, gdn_hbm, outs, sems):
    s = lax.axis_index("section")
    rows, width = on_hbm.shape
    gives = [
        pltpu.make_async_copy(src, dst, sems.at[i])
        for i, (src, dst) in enumerate(
            ((outs.at[0], on_hbm), (outs.at[1], back_hbm), (ggu, ggu_hbm), (gdn, gdn_hbm))
        )
    ]
    for give in gives[2:]:
        give.start()
    lane = lax.broadcasted_iota(jnp.int32, (rows, rows), 1)
    for t in range(2):
        there = jnp.broadcast_to(metar[t, 0:1, :], (rows, rows)).T
        pick = jnp.where(there == lane.astype(F32), 1.0, 0.0).astype(BF16)
        scale = jnp.broadcast_to(metar[t, 8:9, :], (rows, rows)).T[:, 0:1]
        edge = s == (0, 7)[t]

        @pl.loop(0, width // COLS)
        def _(j):
            cols = pl.ds(pl.multiple_of(j * COLS, COLS), COLS)
            mixed = jnp.dot(pick, slots[t, :, cols], preferred_element_type=F32)
            if t == 0:
                mixed = mixed * scale
            outs[t, :, cols] = jnp.where(edge, 0.0, mixed).astype(BF16)

        gives[t].start()
    for give in gives:
        give.wait()


def shards(tokens, cotangent, routes, gates, gate_up, down):
    rows, width = tokens.shape[1:]
    quarter = down.shape[2]
    both = 2 * quarter
    hbm = pl.BlockSpec(memory_space=pl.ANY)
    in_hbm = lambda x: pltpu.with_memory_space_constraint(x, pltpu.HBM)
    vmem = pl.BlockSpec(memory_space=pltpu.VMEM)
    shape = lambda *dims: jax.ShapeDtypeStruct(dims, BF16)
    flops = 2 * 9 * 4 * rows * quarter * width
    handed, metar, ggu, gdn = pl.pallas_call(
        kernel,
        out_shape=(
            pltpu.VMEM((2, rows, width), BF16),
            pltpu.VMEM((2, 16, rows), F32),
            pltpu.VMEM((both, width), BF16),
            pltpu.VMEM((quarter, width), BF16),
        ),
        in_specs=[hbm] * 6,
        out_specs=[vmem] * 4,
        scratch_shapes=[
            pltpu.VMEM((rows, width), BF16),
            pltpu.VMEM((rows, width), BF16),
            pltpu.VMEM((both, width), BF16),
            pltpu.VMEM((quarter, width), BF16),
            pltpu.VMEM((6, 1, rows), jnp.int32),
            pltpu.VMEM((6, 1, rows), F32),
            pltpu.VMEM((2, rows, width), BF16),
            pltpu.VMEM((2, 4 * rows, width), BF16),
            pltpu.VMEM((2, 4 * rows, width), BF16),
            pltpu.VMEM((2, rows, width), BF16),
            pltpu.VMEM((2, 2, rows, width), BF16),
            pltpu.VMEM((2, rows, width), BF16),
            pltpu.VMEM((16, rows), F32),
            pltpu.VMEM((4 * rows, quarter), F32),
            pltpu.VMEM((4 * rows, both), F32),
            pltpu.SemaphoreType.DMA((6,)),
            pltpu.SemaphoreType.DMA((COPIES,)),
            pltpu.SemaphoreType.DMA((COPIES,)),
        ],
        compiler_params=pltpu.CompilerParams(
            collective_id=0, has_side_effects=True, vmem_limit_bytes=40 * 2**20
        ),
        cost_estimate=pl.CostEstimate(flops=flops, bytes_accessed=12 * 2**20, transcendentals=0),
    )(
        in_hbm(tokens[0]), in_hbm(cotangent[0]),
        in_hbm(routes.transpose(2, 0, 1)), in_hbm(gates.transpose(2, 0, 1)),
        in_hbm(gate_up.reshape(both, width)), in_hbm(down.reshape(quarter, width)),
    )
    on, back, ggu, gdn = pl.pallas_call(
        place_rows,
        out_shape=(shape(rows, width), shape(rows, width), shape(both, width), shape(quarter, width)),
        in_specs=[vmem] * 4,
        out_specs=[hbm] * 4,
        scratch_shapes=[pltpu.VMEM((2, rows, width), BF16), pltpu.SemaphoreType.DMA((4,))],
        compiler_params=pltpu.CompilerParams(vmem_limit_bytes=24 * 2**20),
        cost_estimate=pl.CostEstimate(flops=8 * 128 * rows * width, bytes_accessed=11 * 2**20, transcendentals=0),
    )(*(pltpu.with_memory_space_constraint(x, pltpu.VMEM) for x in (handed, metar, ggu, gdn)))
    return (
        on[None],
        back[None],
        ggu.reshape(gate_up.shape),
        gdn.reshape(down.shape),
    )


def solution(mesh):
    in_specs = (
        P("section", ("dp", "expert"), None),
        P("section", ("dp", "expert"), None),
        P("section", ("dp", "expert"), None),
        P("section", ("dp", "expert"), None),
        P("section", "expert", None, "dp", None),
        P("section", "expert", "dp", None),
    )
    out_specs = (
        P("section", ("dp", "expert"), None),
        P("section", ("dp", "expert"), None),
        P("section", "expert", None, "dp", None),
        P("section", "expert", "dp", None),
    )
    return jax.shard_map(shards, mesh=mesh, in_specs=in_specs, out_specs=out_specs, check_vma=False)
```

```python
import functools

import jax
import jax.numpy as jnp
from jax import lax
from jax.experimental import pallas as pl
from jax.experimental.pallas import tpu as pltpu
from jax.sharding import PartitionSpec as P

MESH = pl.DeviceIdType.MESH
F32 = jnp.float32
BF16 = jnp.bfloat16
NT = (((1,), (1,)), ((), ()))
COLS = 512
WIDE = 640
PIECES = ((0,), (1,), (2,), (3,), (4,), (5,), (6,), (7,))
COPIES = 7 + 10 * len(PIECES) + 16 + 2
ORDER = (
    "Z1", "Z2", "Z3", "Z4", "Z5", "Z6", "Z7", "A0", "A1", "B0", "P0", "A2",
    "B1", "C0", "R0", "M0", "A3", "B2", "C1", "R1", "F0", "M1", "A4", "B3",
    "C2", "R2", "F1", "M2", "A5", "B4", "C3", "R3", "F2", "M3", "A6", "B5",
    "C4", "R4", "F3", "M4", "A7", "B6", "C5", "R5", "F4", "M5", "B7", "C6",
    "R6", "F5", "M6", "C7", "R7", "F6",  "M7", "F7", "D0", "G0",
)


def flipped(index, bits):
    out = index
    for b in range(3):
        if bits >> b & 1:
            out = out + (1 << b) * (1 - 2 * ((index // (1 << b)) % 2))
    return out


def kernel(
    tok_hbm, cot_hbm, routes_hbm, gates_hbm, gu_hbm, dn_hbm,
    rsec, metar, ggu, gdn,
    tok, cot, wgu, wdn, routes_ref, gates_ref, pk, xs, part, rdiag, rown, fin, metas,
    hid, gr, lsem, ssem, rsem,
):
    s = lax.axis_index("section")
    q = lax.axis_index("dp")
    e = lax.axis_index("expert")
    nxt, prv = (s + 1) % 8, (s + 7) % 8
    up, dwn = (q + 1) % 4, (q + 3) % 4
    rows, width = tok.shape
    quarter = wdn.shape[0]
    left, right = pl.ds(0, width // 2), pl.ds(width // 2, width // 2)

    barrier = pltpu.get_barrier_semaphore()
    peers = [(s, q, flipped(e, k)) for k in range(1, 8)]
    peers += [(s, up, e), (s, dwn, e)]
    peers += [(t, q, flipped(e, k)) for t in (nxt, prv) for k in range(8)]
    for peer in peers:
        pl.semaphore_signal(barrier, inc=1, device_id=peer, device_id_type=MESH)

    loads = [
        pltpu.make_async_copy(src, dst, lsem.at[i])
        for i, (src, dst) in enumerate(
            (
                (tok_hbm, tok), (cot_hbm, cot), (gu_hbm, wgu), (dn_hbm, wdn),
                (routes_hbm, routes_ref), (gates_hbm, gates_ref),
            )
        )
    ]
    for i in (4, 5, 0, 1, 2, 3):
        loads[i].start()
    used = []

    def copy(src, dst, peer):
        i = len(used)
        c = pltpu.make_async_remote_copy(
            src_ref=src, dst_ref=dst, send_sem=ssem.at[i], recv_sem=rsem.at[i],
            device_id=peer, device_id_type=MESH,
        )
        used.append(c)
        return c

    def tiles(body, first=0, last=width, step=COLS):
        @pl.loop(first // step, last // step)
        def _(j):
            body(pl.ds(pl.multiple_of(j * step, step), step))

    start = [64 * sum(len(p) for p in PIECES[:c]) for c in range(len(PIECES))]
    size = [16 * len(p) for p in PIECES]

    def block(r, c):
        return pl.ds(start[c] + r * size[c], size[c])

    def slots(c):
        return pl.ds(16 * PIECES[c][0], size[c])

    both = pl.ds(0, 2)
    zc = {}
    own, onward, far, near, merged, final = [], [], [], [], [], {}
    for c, piece in enumerate(PIECES):
        for i, k in enumerate(piece):
            at = pl.ds(start[c] + 16 * i, 16)
            if k:
                zc[k] = copy(pk.at[both, pl.ds(k * 16, 16)], xs.at[both, at], (s, q, flipped(e, k)))
    for c in range(len(PIECES)):
        own.append([copy(xs.at[both, block(0, c)], xs.at[both, block(r, c)], (s, y, e)) for y, r in ((up, 3), (dwn, 1))])
        onward.append([
            copy(xs.at[both, block(r, c), h], xs.at[both, block(2, c), h], (s, y, e))
            for y, r, h in ((up, 3, left), (dwn, 1, right))
        ])
        far.append([
            copy(part.at[both, block(2, c), h], rdiag.at[both, slots(c), h], (s, y, e))
            for y, h in ((up, left), (dwn, right))
        ])
        near.append([
            copy(part.at[both, block(r, c), h], rown.at[i, both, slots(c), h], (s, y, e))
            for i, (y, r, h) in enumerate(((up, 1, right), (dwn, 3, left)))
        ])
        merged.append([
            copy(part.at[both, block(r, c), h], rown.at[i, both, slots(c), h], (s, y, e))
            for i, (y, r, h) in enumerate(((up, 1, left), (dwn, 3, right)))
        ])
    for t in range(2):
        for k in range(8):
            at = pl.ds(k * 16, 16)
            final[t, k] = copy(fin.at[t, at], rsec.at[t, at], ((nxt, prv)[t], q, flipped(e, k)))
    meta = [copy(metas, metar.at[t], ((nxt, prv)[t], q, e)) for t in range(2)]
    assert len(used) == COPIES

    loads[4].wait()
    loads[5].wait()
    in_window = routes_ref[...] < 8
    expert_of = jnp.sum(jnp.where(in_window, routes_ref[...], 0), 0)
    present = jnp.sum(jnp.where(in_window, 1, 0), 0) > 0
    weight = jnp.sum(jnp.where(in_window, gates_ref[...], 0.0), 0)
    lane = lax.broadcasted_iota(jnp.int32, (rows, rows), 1)
    sub = lax.broadcasted_iota(jnp.int32, (rows, rows), 0)
    member = jnp.where((expert_of == sub[0:16]) & present, 1.0, 0.0)
    earlier = jnp.where(sub < lane, 1.0, 0.0).astype(BF16)
    before = jnp.dot(member.astype(BF16), earlier, preferred_element_type=F32)
    slot = jnp.sum(before * member, 0, keepdims=True)
    column = expert_of ^ e
    place = jnp.where(present, column.astype(F32) * 16.0 + slot, -1.0)
    metas[0:8, :] = jnp.broadcast_to(place, (8, rows))
    metas[8:16, :] = jnp.broadcast_to(weight, (8, rows))
    select = jnp.where(place == sub.astype(F32), 1.0, 0.0).astype(BF16)
    scale_here = jnp.broadcast_to(weight, (rows, rows)).T[:, 0:1]

    for t in range(2):
        loads[t].wait()

        @tiles
        def _(cols):
            values = tok[:, cols] if t == 0 else (cot[:, cols].astype(F32) * scale_here).astype(BF16)
            packed = jnp.dot(select, values, preferred_element_type=F32).astype(BF16)
            pk[t, :, cols] = packed
            xs[t, 0:16, cols] = packed[0:16, :]

    pl.semaphore_wait(barrier, len(peers))

    def send_out(c):
        for k in PIECES[c]:
            if k:
                zc[k].start()

    def spread(c):
        for k in PIECES[c]:
            if k:
                zc[k].wait_recv()
        for y in own[c]:
            y.start()

    def pass_on(c):
        for i in range(2):
            own[c][i].wait_recv()
            onward[c][i].start()

    def compute(c):
        for y in onward[c]:
            y.wait_recv()
        span = pl.ds(start[c], 4 * size[c])
        pre = lax.dot_general(xs[0, span, :], wgu[...], NT, preferred_element_type=F32)
        gate, upper = pre[:, :quarter], pre[:, quarter:]
        sig = jax.nn.sigmoid(gate)
        activated = gate * sig
        hidden = activated * upper
        hid[span, :] = hidden
        hidden = hidden.astype(BF16)
        hg = lax.dot_general(xs[1, span, :], wdn[...], NT, preferred_element_type=F32)
        gg = hg * upper * (sig * (1.0 + gate * (1.0 - sig)))
        ug = hg * activated
        gr[span, :quarter] = gg
        gr[span, quarter:] = ug
        gg, ug = gg.astype(BF16), ug.astype(BF16)

        @tiles
        def _(cols):
            part[0, span, cols] = jnp.dot(hidden, wdn[:, cols], preferred_element_type=F32).astype(BF16)
            into = jnp.dot(gg, wgu[:quarter, cols], preferred_element_type=F32)
            into += jnp.dot(ug, wgu[quarter:, cols], preferred_element_type=F32)
            part[1, span, cols] = into.astype(BF16)

    def reduce(c):
        for y in (*far[c], *near[c]):
            y.start()

    def merge(c):
        for i, (r, first, last) in enumerate(((1, 0, width // 2), (3, width // 2, width))):
            far[c][i].wait_recv()
            mine, theirs = block(r, c), slots(c)

            @functools.partial(tiles, first=first, last=last, step=WIDE)
            def _(cols):
                for t in range(2):
                    total = part[t, mine, cols].astype(F32) + rdiag[t, theirs, cols].astype(F32)
                    part[t, mine, cols] = total.astype(BF16)

            merged[c][i].start()

    def finish(c):
        for y in (*near[c], *merged[c]):
            y.wait_recv()
        mine, span = block(0, c), slots(c)

        @functools.partial(tiles, step=WIDE)
        def _(cols):
            for t in range(2):
                total = part[t, mine, cols].astype(F32) + rown[0, t, span, cols].astype(F32)
                fin[t, span, cols] = (total + rown[1, t, span, cols].astype(F32)).astype(BF16)

        for k in PIECES[c]:
            for t in range(2):
                final[t, k].start()

    def grad_down(_):
        flat = hid[...].T.astype(BF16)

        @tiles
        def _(cols):
            gdn[:, cols] = jnp.dot(flat, xs[1, :, cols], preferred_element_type=F32).astype(BF16)


    def grad_gate_up(_):
        for top in (0, quarter):
            flat = gr[:, top : top + quarter].T.astype(BF16)

            @tiles
            def _(cols):
                ggu[top : top + quarter, cols] = jnp.dot(flat, xs[0, :, cols], preferred_element_type=F32).astype(BF16)


    def ready(_):
        for m in meta:
            m.start()
        for load in loads[2:4]:
            load.wait()

    steps = {
        "Z": send_out, "A": spread, "B": pass_on, "C": compute, "R": reduce, "M": merge, "F": finish,
        "D": grad_down, "G": grad_gate_up, "P": ready,
    }
    for step in ORDER:
        steps[step[0]](int(step[1:]))

    for c in (*meta, *final.values()):
        c.wait_recv()
    for c in used:
        c.wait_send()


def place_rows(slots, metar, ggu, gdn, on_hbm, back_hbm, ggu_hbm, gdn_hbm, outs, sems):
    s = lax.axis_index("section")
    rows, width = on_hbm.shape
    gives = [
        pltpu.make_async_copy(src, dst, sems.at[i])
        for i, (src, dst) in enumerate(
            ((outs.at[0], on_hbm), (outs.at[1], back_hbm), (ggu, ggu_hbm), (gdn, gdn_hbm))
        )
    ]
    for give in gives[2:]:
        give.start()
    lane = lax.broadcasted_iota(jnp.int32, (rows, rows), 1)
    for t in range(2):
        there = jnp.broadcast_to(metar[t, 0:1, :], (rows, rows)).T
        pick = jnp.where(there == lane.astype(F32), 1.0, 0.0).astype(BF16)
        scale = jnp.broadcast_to(metar[t, 8:9, :], (rows, rows)).T[:, 0:1]
        edge = s == (0, 7)[t]

        @pl.loop(0, width // COLS)
        def _(j):
            cols = pl.ds(pl.multiple_of(j * COLS, COLS), COLS)
            mixed = jnp.dot(pick, slots[t, :, cols], preferred_element_type=F32)
            if t == 0:
                mixed = mixed * scale
            outs[t, :, cols] = jnp.where(edge, 0.0, mixed).astype(BF16)

        gives[t].start()
    for give in gives:
        give.wait()


def shards(tokens, cotangent, routes, gates, gate_up, down):
    rows, width = tokens.shape[1:]
    quarter = down.shape[2]
    both = 2 * quarter
    hbm = pl.BlockSpec(memory_space=pl.ANY)
    in_hbm = lambda x: pltpu.with_memory_space_constraint(x, pltpu.HBM)
    vmem = pl.BlockSpec(memory_space=pltpu.VMEM)
    shape = lambda *dims: jax.ShapeDtypeStruct(dims, BF16)
    flops = 2 * 9 * 4 * rows * quarter * width
    handed, metar, ggu, gdn = pl.pallas_call(
        kernel,
        out_shape=(
            pltpu.VMEM((2, rows, width), BF16),
            pltpu.VMEM((2, 16, rows), F32),
            pltpu.VMEM((both, width), BF16),
            pltpu.VMEM((quarter, width), BF16),
        ),
        in_specs=[hbm] * 6,
        out_specs=[vmem] * 4,
        scratch_shapes=[
            pltpu.VMEM((rows, width), BF16),
            pltpu.VMEM((rows, width), BF16),
            pltpu.VMEM((both, width), BF16),
            pltpu.VMEM((quarter, width), BF16),
            pltpu.VMEM((6, 1, rows), jnp.int32),
            pltpu.VMEM((6, 1, rows), F32),
            pltpu.VMEM((2, rows, width), BF16),
            pltpu.VMEM((2, 4 * rows, width), BF16),
            pltpu.VMEM((2, 4 * rows, width), BF16),
            pltpu.VMEM((2, rows, width), BF16),
            pltpu.VMEM((2, 2, rows, width), BF16),
            pltpu.VMEM((2, rows, width), BF16),
            pltpu.VMEM((16, rows), F32),
            pltpu.VMEM((4 * rows, quarter), F32),
            pltpu.VMEM((4 * rows, both), F32),
            pltpu.SemaphoreType.DMA((6,)),
            pltpu.SemaphoreType.DMA((COPIES,)),
            pltpu.SemaphoreType.DMA((COPIES,)),
        ],
        compiler_params=pltpu.CompilerParams(
            collective_id=0, has_side_effects=True, vmem_limit_bytes=40 * 2**20
        ),
        cost_estimate=pl.CostEstimate(flops=flops, bytes_accessed=12 * 2**20, transcendentals=0),
    )(
        in_hbm(tokens[0]), in_hbm(cotangent[0]),
        in_hbm(routes.transpose(2, 0, 1)), in_hbm(gates.transpose(2, 0, 1)),
        in_hbm(gate_up.reshape(both, width)), in_hbm(down.reshape(quarter, width)),
    )
    on, back, ggu, gdn = pl.pallas_call(
        place_rows,
        out_shape=(shape(rows, width), shape(rows, width), shape(both, width), shape(quarter, width)),
        in_specs=[vmem] * 4,
        out_specs=[hbm] * 4,
        scratch_shapes=[pltpu.VMEM((2, rows, width), BF16), pltpu.SemaphoreType.DMA((4,))],
        compiler_params=pltpu.CompilerParams(vmem_limit_bytes=24 * 2**20),
        cost_estimate=pl.CostEstimate(flops=8 * 128 * rows * width, bytes_accessed=11 * 2**20, transcendentals=0),
    )(*(pltpu.with_memory_space_constraint(x, pltpu.VMEM) for x in (handed, metar, ggu, gdn)))
    return (
        on[None],
        back[None],
        ggu.reshape(gate_up.shape),
        gdn.reshape(down.shape),
    )


def solution(mesh):
    in_specs = (
        P("section", ("dp", "expert"), None),
        P("section", ("dp", "expert"), None),
        P("section", ("dp", "expert"), None),
        P("section", ("dp", "expert"), None),
        P("section", "expert", None, "dp", None),
        P("section", "expert", "dp", None),
    )
    out_specs = (
        P("section", ("dp", "expert"), None),
        P("section", ("dp", "expert"), None),
        P("section", "expert", None, "dp", None),
        P("section", "expert", "dp", None),
    )
    return jax.shard_map(shards, mesh=mesh, in_specs=in_specs, out_specs=out_specs, check_vma=False)
```
